32 devices in a mesh: replica: 2 (over x), node: 2 (over core), local: 8 (over z, y).
Axes of the slice: x: 2, y: 2, z: 4, core: 2. Of those that a mesh axis runs over, the one named last changes fastest.
Arguments:
- hidden: bfloat16 [384, 7168], P(('replica', 'node', 'local')), parts along dimension 0, may hold values from -48 to 48
- norm_gain: float32 [7168], replicated, may hold values from 0.25 to 1.75
- expert_ids: int32 [384, 2], P(('replica', 'node', 'local')), parts along dimension 0, may hold values from 0 to 7, all different within a row; in each aligned block of 12 rows (0 to 11, 12 to 23, ...) at most 4 rows name the same one
- gate_weight: float32 [384, 2], P(('replica', 'node', 'local')), parts along dimension 0, may hold values from 0.2 to 1
- gate_proj: bfloat16 [7168, 16384], P(None, ('node', 'local')), may hold values from -0.0625 to 0.0625
- up_proj: bfloat16 [7168, 16384], P(None, ('node', 'local')), may hold values from -0.0625 to 0.0625
- down_proj: bfloat16 [16384, 7168], P(('node', 'local')), may hold values from -0.125 to 0.125
Outputs:
- mixed: bfloat16 [384, 7168], P(('replica', 'node', 'local')), parts along dimension 0
The draws below stay inside these ranges and needn't reach their ends.
There are 2 independent parts, one for each index of `replica`. The reference program is written for one: setup_inputs(seed, part) draws one part's arguments, and reference() takes and returns one part's arrays. A program takes and returns all parts, laid end to end along the dimension named above; an argument that names none is the same for every part. Nothing has to cross between parts.
Inputs may be any that keep to these rules, and one draw needn't show every extreme that they name: `expert_ids`: each row names 2 different experts. Within each device's block of 12 rows no expert is named by more than 4 rows, and some block reaches that.
All inputs are finite; a program needn't handle non-finite values.
Results may differ from the reference program's by a relative error of at most 0.008.
Values may be sent and summed in bfloat16 or wider, within the bound.
A program may use at most 128 MiB of HBM per device.

```python
import math
import jax
import jax.numpy as jnp
import numpy as np
from jax import lax

D = 7168
FFE = 2048
EXP_GROUP = 4
TOPK = 2
ROWS = 12
EXPERTS = 8
CAPACITY = 4
HID_DEV = 1024
TOKENS = 192
N_LOCAL = 8


def draw_hidden(key, part):
    key = jax.random.fold_in(key, 11)
    first_key, second_key, third_key = jax.random.split(key, 3)
    row_scale = jnp.exp(jax.random.uniform(second_key, (TOKENS, 1), minval=-1.2, maxval=1.2))
    col_scale = jnp.exp(jax.random.uniform(third_key, (1, D), minval=-1.2, maxval=1.2))
    base = jnp.clip(jax.random.normal(first_key, (TOKENS, D)), -4.0, 4.0)
    return (base * row_scale * col_scale).astype(jnp.bfloat16)


def level_of(key, dims, cuts, least, largest):
    level = 1.0
    for dim, shards_of in cuts:
        steps = jax.random.uniform(jax.random.fold_in(jax.random.fold_in(key, 6), dim), (shards_of,), jnp.float32, least / len(cuts), largest / len(cuts))
        level = level * jnp.repeat(jnp.exp(steps), dims[dim] // shards_of).reshape((-1,) + (1,) * (len(dims) - 1 - dim))
    return level


def assign_block(own_key, own, number, rows, number_of, top, most, slope):
    sequence = jax.random.permutation(own_key, number_of)
    packed, common = shares(number_of, rows * top, most, slope, True), shares(number_of, rows * top, most, slope, False)
    places = jnp.arange(number_of)

    def named(lengths, rotation):
        used = int((lengths > 0).sum())
        fixed = max(1, used // 4)
        shifted = fixed + (places - fixed + rotation * (used - fixed)) % max(1, number_of - fixed)
        return jnp.zeros((number_of,), jnp.int32).at[sequence[jnp.where(places < fixed, places, shifted)]].set(jnp.asarray(lengths, jnp.int32))

    lengths = jnp.where(number % 4 == 0, named(packed, number // 4), named(common, number - number // 4 - 1))
    mixed = jax.random.permutation(jax.random.fold_in(own, 3), number_of)
    giver, receiver = mixed[0:number_of // 2 * 2:2], mixed[1:number_of // 2 * 2:2]
    margin = jnp.minimum(lengths[giver] - 1, most - lengths[receiver]) // 2
    margin = jnp.where((giver == sequence[0]) | (receiver == sequence[0]) | (lengths[receiver] == 0), 0, jnp.maximum(margin, 0))
    shifted = jax.random.randint(jax.random.fold_in(own, 4), (number_of // 2,), 0, 1 << 20) % (margin + 1)
    lengths = lengths.at[giver].add(-shifted).at[receiver].add(shifted)
    items = jnp.searchsorted(jnp.cumsum(lengths), jnp.arange(rows * top), side="right").astype(jnp.int32)
    grid = items.reshape(top, rows).T
    grid = grid[jax.random.permutation(jax.random.fold_in(own, 1), rows)]
    rotation = jax.random.randint(jax.random.fold_in(own, 2), (rows, 1), 0, top)
    return jnp.take_along_axis(grid, (jnp.arange(top)[None, :] + rotation) % top, axis=1)


def shares(count, total, bound, skew, full):
    weights = [(1 << 20) // math.isqrt(grade ** skew) + 1 for grade in range(1, count + 1)]
    largest = bound if full else min(bound, max(-(-total // count), total * weights[0] // sum(weights)))
    least = 1 if total - largest >= count - 1 else 0
    holding, spare = [largest] + [least] * (count - 1), total - largest - least * (count - 1)
    while spare > 0:
        movable = [i for i in range(1, count) if holding[i] < largest] or [i for i in range(1, count) if holding[i] < bound]
        pool, remaining = sum([weights[i] for i in movable]), spare
        for i in movable:
            extra = min(bound - holding[i], max(1, remaining * weights[i] // pool), spare)
            holding[i] = holding[i] + extra
            spare = spare - extra
    return np.array(holding)


def centred(rng, shape, width, most, cuts=(), kind=jnp.bfloat16):
    factor_of = level_of(rng, shape, cuts, -0.22, 0.18) if cuts else 1.0
    values = jax.random.normal(rng, shape, jnp.float32) * width * factor_of
    return jnp.minimum(jnp.maximum(values, -most), most).astype(kind)


def setup_inputs(seed: int = 0, part: int = 0) -> dict:
    keys = jax.random.split(jax.random.key(seed), 8)
    part_keys = jax.random.split(jax.random.fold_in(keys[7], part), 8)
    hidden = draw_hidden(jax.random.fold_in(jax.random.fold_in(keys[7], part), 71), part)
    norm_gain = jnp.clip(1.0 + 0.15 * jax.random.normal(keys[1], (D,), jnp.float32), 0.25, 1.75)
    expert_ids_keys = jax.random.split(jax.random.fold_in(part_keys[2], 1), TOKENS // ROWS)
    expert_ids_turns = jax.random.permutation(jax.random.fold_in(part_keys[2], 3), TOKENS // ROWS)
    expert_ids = jax.vmap(lambda own, number: assign_block(jax.random.fold_in(part_keys[2], 2), own, number, ROWS, EXPERTS, TOPK, CAPACITY, 2))(expert_ids_keys, expert_ids_turns).reshape((TOKENS, TOPK))
    gate_weight = jnp.clip(0.2 + 0.8 * jax.random.uniform(part_keys[3], (TOKENS, TOPK), jnp.float32) ** level_of(part_keys[3], (TOKENS, TOPK), ((0, 16),), -0.2, 0.2), 0.2, 1.0)
    gate_proj = centred(keys[4], (D, EXPERTS * FFE), D ** -0.5, 0.0625, ((1, 16),))
    up_proj = centred(keys[5], (D, EXPERTS * FFE), D ** -0.5, 0.0625, ((1, 16),))
    down_proj = centred(keys[6], (EXPERTS * FFE, D), FFE ** -0.5, 0.125, ((0, 16),))
    return dict(hidden=hidden, norm_gain=norm_gain, expert_ids=expert_ids, gate_weight=gate_weight, gate_proj=gate_proj, up_proj=up_proj, down_proj=down_proj)


def slot_positions(expert_ids):
    device_count = TOKENS // ROWS
    blocks = expert_ids.reshape(device_count, ROWS * TOPK)
    chosen = (blocks[:, :, None] == jnp.arange(EXPERTS, dtype=jnp.int32)[None, None, :]).astype(jnp.int32)
    before = jnp.cumsum(chosen, axis=1) - chosen
    slot_index = lax.optimization_barrier(jnp.sum(before * chosen, axis=2))
    device_index = jnp.arange(device_count, dtype=jnp.int32)[:, None]
    return (device_index * CAPACITY + slot_index).reshape(TOKENS, TOPK).astype(jnp.int32)

def reference(hidden, norm_gain, expert_ids, gate_weight, gate_proj, up_proj, down_proj):
    values = hidden.astype(jnp.float32)
    row_scale = lax.rsqrt(lax.optimization_barrier(jnp.mean(values * values, axis=1, keepdims=True)) + 1e-06)
    normed = (values * row_scale * norm_gain[None, :]).astype(jnp.bfloat16)
    position = slot_positions(expert_ids)
    buffer_rows = TOKENS // ROWS * CAPACITY
    slot_grid = jnp.arange(buffer_rows, dtype=jnp.int32)
    sharers = N_LOCAL // EXP_GROUP

    def expert_output(expert_index):
        match_grid = (expert_ids == expert_index)[None, :, :] & (position[None, :, :] == slot_grid[:, None, None])
        gather_matrix = jnp.any(match_grid, axis=2).astype(jnp.bfloat16)
        rows_in = jnp.dot(gather_matrix, normed, preferred_element_type=jnp.float32).astype(jnp.bfloat16)
        first_col = (expert_index * FFE).astype(jnp.int32)
        gate_cols = lax.dynamic_slice_in_dim(gate_proj, first_col, FFE, 1)
        up_cols = lax.dynamic_slice_in_dim(up_proj, first_col, FFE, 1)
        gate_part = jnp.dot(rows_in, gate_cols, preferred_element_type=jnp.float32)
        up_part = jnp.dot(rows_in, up_cols, preferred_element_type=jnp.float32)
        active = (jax.nn.silu(gate_part) * up_part).astype(jnp.bfloat16)
        down_rows = lax.dynamic_slice_in_dim(down_proj, first_col, FFE, 0)

        def add_range(total, range_index):
            first_unit = (range_index * HID_DEV).astype(jnp.int32)
            act_slice = lax.dynamic_slice_in_dim(active, first_unit, HID_DEV, 1)
            weight_slice = lax.dynamic_slice_in_dim(down_rows, first_unit, HID_DEV, 0)
            rounded = jnp.dot(act_slice, weight_slice, preferred_element_type=jnp.float32).astype(jnp.bfloat16)
            rounded = lax.optimization_barrier(rounded)
            return (total + rounded.astype(jnp.float32), None)
        start_total = jnp.zeros((buffer_rows, D), jnp.float32)
        total, unused = lax.scan(add_range, start_total, jnp.arange(sharers, dtype=jnp.int32))
        return total.astype(jnp.bfloat16)
    outputs = lax.map(expert_output, jnp.arange(EXPERTS, dtype=jnp.int32))
    flat_outputs = outputs.reshape(EXPERTS * buffer_rows, D)
    row_index = (expert_ids * buffer_rows + position).astype(jnp.int32)
    picked = jnp.take(flat_outputs, row_index, axis=0).astype(jnp.float32)
    mixed = lax.optimization_barrier(jnp.sum(gate_weight[:, :, None] * picked, axis=1))
    return mixed.astype(jnp.bfloat16)
```

```python
import functools

import jax
import jax.numpy as jnp
from jax import lax
from jax.experimental import pallas as pl
from jax.experimental.pallas import tpu as pltpu
from jax.sharding import PartitionSpec as P

EXP_GROUP = 4
CAPACITY = 4
SEGS = 4
PAD_ROWS = 16
MESH = pl.DeviceIdType.MESH
F32 = jnp.float32
BF16 = jnp.bfloat16


def iota(shape, dim):
    return lax.broadcasted_iota(jnp.int32, shape, dim)


def one_hot_shuffle(experts, to_segments):
    rows = experts * SEGS * CAPACITY
    first, second = iota((rows, rows), 0), iota((rows, rows), 1)
    by_segment, by_expert = (first, second) if to_segments else (second, first)
    expert = by_expert // (SEGS * CAPACITY)
    segment = (by_expert // CAPACITY) % SEGS
    slot = by_expert % CAPACITY
    wanted = segment * (experts * CAPACITY) + expert * CAPACITY + slot
    return (by_segment == wanted).astype(F32).astype(BF16)


def kernel(
    dims,
    hidden_ref, gain_ref, ids_ref, weight_ref, gate_hbm, up_hbm, down_hbm,
    out_ref,
    gate_w, up_w, down_w, stacked, picks, mixing, outbox, inbox, rows_in, gate_acc, up_acc,
    part_out, part_in, sum_out, sum_in,
    w_sem, row_send, row_recv, fwd_send, fwd_recv, part_send, part_recv, sum_send, sum_recv,
):
    experts, sharers, chunks, width, row_count, routes = dims
    slots = SEGS * CAPACITY
    flat = experts * slots
    block = experts * CAPACITY
    model_width = hidden_ref.shape[1]
    seg_width = model_width // SEGS
    replica = lax.axis_index("replica")
    node = lax.axis_index("node")
    local = lax.axis_index("local")
    sharer = lax.rem(local, sharers)
    mine = node * EXP_GROUP + lax.div(local, sharers)

    def at_expert(expert, share):
        return (
            replica,
            lax.div(expert, EXP_GROUP),
            lax.rem(expert, EXP_GROUP) * sharers + share,
        )

    def other_expert(step):
        return lax.rem(mine + step, experts)

    def other_sharer(step):
        return lax.rem(sharer + step, sharers)

    def weight_copy(kind, chunk, seg):
        at = seg * seg_width + chunk * width
        if kind == 2:
            source = down_hbm.at[:, pl.ds(at, width)]
            target = down_w.at[chunk, :, pl.ds(seg * width, width)]
        else:
            source = (gate_hbm, up_hbm)[kind].at[pl.ds(at, width), :]
            target = (gate_w, up_w)[kind].at[chunk, pl.ds(seg * width, width), :]
        return pltpu.make_async_copy(source, target, w_sem.at[kind, chunk, seg])

    for chunk in range(chunks):
        for kind in range(2):
            for seg in range(SEGS):
                weight_copy(kind, chunk, seg).start()
    for chunk in range(chunks):
        for seg in range(SEGS):
            weight_copy(2, chunk, seg).start()

    barrier = pltpu.get_barrier_semaphore()
    for step in range(1, experts):
        pl.semaphore_signal(
            barrier, inc=1, device_id=at_expert(other_expert(step), sharer), device_id_type=MESH
        )
    for step in range(1, sharers):
        pl.semaphore_signal(
            barrier, inc=1, device_id=at_expert(mine, other_sharer(step)), device_id_type=MESH
        )

    lane_expert = iota((row_count, flat), 1) // slots
    lane_slot = iota((row_count, flat), 1) % CAPACITY
    chosen = jnp.zeros((row_count, flat), F32)
    weights = jnp.zeros((row_count, flat), F32)
    for route in range(routes):
        named = ids_ref[:, route:route + 1] == lane_expert
        chosen = jnp.where(named, 1.0, chosen)
        weights = jnp.where(named, weight_ref[:, route:route + 1], weights)
    picks[...] = jnp.zeros_like(picks)
    mixing[...] = jnp.zeros_like(mixing)
    before = jnp.zeros((1, flat), F32)
    lane_slot_f = (iota((1, flat), 1) % CAPACITY).astype(F32)
    lane_seg = (iota((1, flat), 1) // CAPACITY) % SEGS
    for row in range(row_count):
        chosen_row = chosen[row:row + 1, :]
        hit = jnp.where(before == lane_slot_f, chosen_row, 0.0)
        scaled = hit * weights[row:row + 1, :]
        for seg in range(SEGS):
            here = lane_seg == seg
            picks[pl.ds(seg * PAD_ROWS + row, 1), :] = jnp.where(here, hit, 0.0)
            mixing[pl.ds(seg * PAD_ROWS + row, 1), :] = jnp.where(here, scaled, 0.0)
        before = before + chosen_row

    values = hidden_ref[...].astype(F32)
    scale = lax.rsqrt(jnp.mean(values * values, axis=1, keepdims=True) + 1e-06)
    normed = values * scale * gain_ref[...]
    stacked[...] = jnp.zeros_like(stacked)
    for seg in range(SEGS):
        stacked[pl.ds(seg * PAD_ROWS, row_count), :] = normed[
            :, seg * seg_width:(seg + 1) * seg_width
        ]
    picked = picks[...].astype(BF16)

    def row_copy(chunk, source_expert, target_expert):
        return pltpu.make_async_remote_copy(
            src_ref=outbox.at[chunk, target_expert],
            dst_ref=inbox.at[chunk, sharer, source_expert],
            send_sem=row_send.at[chunk, target_expert],
            recv_sem=row_recv.at[chunk, source_expert],
            device_id=at_expert(target_expert, sharer),
            device_id_type=MESH,
        )

    def forward_copy(chunk, source_share, target_share):
        return pltpu.make_async_remote_copy(
            src_ref=inbox.at[chunk, source_share],
            dst_ref=inbox.at[chunk, source_share],
            send_sem=fwd_send.at[chunk, target_share],
            recv_sem=fwd_recv.at[chunk, source_share],
            device_id=at_expert(mine, target_share),
            device_id_type=MESH,
        )

    def part_copy(chunk, source_share, target_share):
        return pltpu.make_async_remote_copy(
            src_ref=part_out.at[chunk, target_share],
            dst_ref=part_in.at[chunk, source_share],
            send_sem=part_send.at[chunk, target_share],
            recv_sem=part_recv.at[chunk, source_share],
            device_id=at_expert(mine, target_share),
            device_id_type=MESH,
        )

    def sum_copy(chunk, source_expert, target_expert):
        return pltpu.make_async_remote_copy(
            src_ref=sum_out.at[chunk, target_expert],
            dst_ref=sum_in.at[chunk, source_expert],
            send_sem=sum_send.at[chunk, target_expert],
            recv_sem=sum_recv.at[chunk, source_expert],
            device_id=at_expert(target_expert, sharer),
            device_id_type=MESH,
        )

    pl.semaphore_wait(barrier, experts - 1 + sharers - 1)

    for chunk in range(chunks):
        rows = stacked[:, chunk * width:(chunk + 1) * width].astype(BF16)
        placed = lax.dot_general(
            picked, rows, (((0,), (0,)), ((), ())), preferred_element_type=F32
        ).astype(BF16)
        outbox[chunk] = placed.reshape(experts, slots, width)
        for step in range(1, experts):
            row_copy(chunk, mine, other_expert(step)).start()
        inbox[chunk, sharer, mine] = outbox[chunk, mine]

    to_segments = one_hot_shuffle(experts, True)
    to_experts = one_hot_shuffle(experts, False)

    def gather_rows(chunk):
        for step in range(1, experts):
            source = other_expert(step)
            row_copy(chunk, source, source).wait_recv()
        for step in range(1, sharers):
            forward_copy(chunk, sharer, other_sharer(step)).start()

    def expand(chunk):
        for step in range(1, sharers):
            source = other_sharer(step)
            forward_copy(chunk, source, source).wait_recv()
        for share in range(sharers):
            ordered = jnp.dot(
                to_segments,
                inbox[chunk, share].reshape(flat, width),
                preferred_element_type=F32,
            ).astype(BF16)
            for seg in range(SEGS):
                rows_in[share * block:(share + 1) * block, seg * width:(seg + 1) * width] = (
                    ordered[seg * block:(seg + 1) * block]
                )
        for kind, matrix, total in ((0, gate_w, gate_acc), (1, up_w, up_acc)):
            for seg in range(SEGS):
                weight_copy(kind, chunk, seg).wait()
            product = jnp.dot(rows_in[...], matrix[chunk], preferred_element_type=F32)
            if chunk == 0:
                total[...] = product
            else:
                total[...] += product

    for chunk in range(chunks):
        gather_rows(chunk)
        if chunk >= 1:
            expand(chunk - 1)
    expand(chunks - 1)

    gate = gate_acc[...]
    active = (gate / (1.0 + jnp.exp(-gate)) * up_acc[...]).astype(BF16)

    mix = mixing[...]
    mix_high = mix.astype(BF16)
    rest = mix - mix_high.astype(F32)
    mix_mid = rest.astype(BF16)
    mix_low = (rest - mix_mid.astype(F32)).astype(BF16)
    mix_parts = jnp.concatenate([mix_high, mix_mid, mix_low], axis=0)

    def contract(chunk):
        for seg in range(SEGS):
            weight_copy(2, chunk, seg).wait()
        product = jnp.dot(active, down_w[chunk], preferred_element_type=F32).astype(BF16)
        for share in range(sharers):
            for seg in range(SEGS):
                part_out[chunk, share, seg * block:(seg + 1) * block, :] = product[
                    share * block:(share + 1) * block, seg * width:(seg + 1) * width
                ]
        for step in range(1, sharers):
            part_copy(chunk, sharer, other_sharer(step)).start()

    def add_parts(chunk):
        total = part_out[chunk, sharer].astype(F32)
        for step in range(1, sharers):
            source = other_sharer(step)
            part_copy(chunk, source, source).wait_recv()
            total = total + part_in[chunk, source].astype(F32)
        ordered = jnp.dot(to_experts, total.astype(BF16), preferred_element_type=F32).astype(BF16)
        sum_out[chunk] = ordered.reshape(experts, slots, width)
        for step in range(1, experts):
            sum_copy(chunk, mine, other_expert(step)).start()
        sum_in[chunk, mine] = sum_out[chunk, mine]

    def mix_rows(chunk):
        for step in range(1, experts):
            source = other_expert(step)
            sum_copy(chunk, source, source).wait_recv()
        arrived = sum_in[chunk].reshape(flat, width)
        terms = jnp.dot(mix_parts, arrived, preferred_element_type=F32)
        size = SEGS * PAD_ROWS
        mixed = terms[:size] + terms[size:2 * size] + terms[2 * size:]
        for seg in range(SEGS):
            at = seg * seg_width + chunk * width
            out_ref[:, at:at + width] = mixed[
                seg * PAD_ROWS:seg * PAD_ROWS + row_count
            ].astype(BF16)

    for turn in range(chunks + 4):
        if turn < chunks:
            contract(turn)
        if 0 <= turn - 1 < chunks:
            add_parts(turn - 1)
        if 0 <= turn - 4 < chunks:
            mix_rows(turn - 4)

    for chunk in range(chunks):
        for step in range(1, experts):
            row_copy(chunk, mine, other_expert(step)).wait_send()
            sum_copy(chunk, mine, other_expert(step)).wait_send()
        for step in range(1, sharers):
            forward_copy(chunk, sharer, other_sharer(step)).wait_send()
            part_copy(chunk, sharer, other_sharer(step)).wait_send()


def shards(hidden, norm_gain, expert_ids, gate_weight, gate_proj, up_proj, down_proj):
    experts = EXP_GROUP * lax.axis_size("node")
    sharers = lax.axis_size("local") // EXP_GROUP
    row_count, model_width = hidden.shape
    routes = expert_ids.shape[1]
    units = gate_proj.shape[1]
    seg_width = model_width // SEGS
    width = 256
    chunks = seg_width // width
    slots = SEGS * CAPACITY
    flat = experts * slots
    block = experts * CAPACITY
    vmem = pl.BlockSpec(memory_space=pltpu.VMEM)
    anywhere = pl.BlockSpec(memory_space=pl.ANY)
    dma = pltpu.SemaphoreType.DMA
    return pl.pallas_call(
        functools.partial(kernel, (experts, sharers, chunks, width, row_count, routes)),
        out_shape=jax.ShapeDtypeStruct((row_count, model_width), BF16),
        in_specs=[vmem] * 4 + [anywhere] * 3,
        out_specs=vmem,
        scratch_shapes=[
            pltpu.VMEM((chunks, SEGS * width, units), BF16),
            pltpu.VMEM((chunks, SEGS * width, units), BF16),
            pltpu.VMEM((chunks, units, SEGS * width), BF16),
            pltpu.VMEM((SEGS * PAD_ROWS, seg_width), F32),
            pltpu.VMEM((SEGS * PAD_ROWS, flat), F32),
            pltpu.VMEM((SEGS * PAD_ROWS, flat), F32),
            pltpu.VMEM((chunks, experts, slots, width), BF16),
            pltpu.VMEM((chunks, sharers, experts, slots, width), BF16),
            pltpu.VMEM((sharers * block, SEGS * width), BF16),
            pltpu.VMEM((sharers * block, units), F32),
            pltpu.VMEM((sharers * block, units), F32),
            pltpu.VMEM((chunks, sharers, SEGS * block, width), BF16),
            pltpu.VMEM((chunks, sharers, SEGS * block, width), BF16),
            pltpu.VMEM((chunks, experts, slots, width), BF16),
            pltpu.VMEM((chunks, experts, slots, width), BF16),
            dma((3, chunks, SEGS)),
            dma((chunks, experts)),
            dma((chunks, experts)),
            dma((chunks, sharers)),
            dma((chunks, sharers)),
            dma((chunks, sharers)),
            dma((chunks, sharers)),
            dma((chunks, experts)),
            dma((chunks, experts)),
        ],
        compiler_params=pltpu.CompilerParams(
            collective_id=0, has_side_effects=True, vmem_limit_bytes=58 * 1024 * 1024
        ),
        name="expert_layer",
    )(hidden, norm_gain.reshape(1, model_width), expert_ids, gate_weight, gate_proj, up_proj, down_proj)


def solution(mesh):
    return jax.shard_map(
        shards,
        mesh=mesh,
        in_specs=(
            P(("replica", "node", "local"), None),
            P(),
            P(("replica", "node", "local"), None),
            P(("replica", "node", "local"), None),
            P(None, ("node", "local")),
            P(None, ("node", "local")),
            P(("node", "local"), None),
        ),
        out_specs=P(("replica", "node", "local"), None),
        check_vma=False,
    )
```

```python
import functools

import jax
import jax.numpy as jnp
from jax import lax
from jax.experimental import pallas as pl
from jax.experimental.pallas import tpu as pltpu
from jax.sharding import PartitionSpec as P

EXP_GROUP = 4
CAPACITY = 4
SEGS = 4
PAD_ROWS = 16
IN_FLIGHT = 2
ADD_LAG = 2
MIX_LAG = 4
ROW_CUTS = (7, 7)
OUT_CUTS = (4, 4, 4, 2)
MESH = pl.DeviceIdType.MESH
F32 = jnp.float32
BF16 = jnp.bfloat16


def iota(shape, dim):
    return lax.broadcasted_iota(jnp.int32, shape, dim)


def spans(cuts, whole):
    unit, at, out = whole // sum(cuts), 0, []
    for cut in cuts:
        out.append((at, cut * unit))
        at += cut * unit
    return out


def one_hot_shuffle(experts, to_segments):
    rows = experts * SEGS * CAPACITY
    first, second = iota((rows, rows), 0), iota((rows, rows), 1)
    by_segment, by_expert = (first, second) if to_segments else (second, first)
    expert = by_expert // (SEGS * CAPACITY)
    segment = (by_expert // CAPACITY) % SEGS
    slot = by_expert % CAPACITY
    wanted = segment * (experts * CAPACITY) + expert * CAPACITY + slot
    return (by_segment == wanted).astype(F32).astype(BF16)


def kernel(
    dims,
    hidden_ref, gain_ref, ids_ref, weight_ref, gate_hbm, up_hbm, down_hbm,
    out_ref,
    gate_w, up_w, down_w, stacked, mixing, outbox, inbox, rows_in, gate_acc, up_acc,
    part_out, part_in, sum_out, sum_in,
    w_sem, row_send, row_recv, fwd_send, part_send, part_recv, sum_send, sum_recv,
):
    experts, sharers, row_count, routes = dims
    slots = SEGS * CAPACITY
    flat = experts * slots
    block = experts * CAPACITY
    model_width = hidden_ref.shape[1]
    seg_width = model_width // SEGS
    row_spans, out_spans = spans(ROW_CUTS, seg_width), spans(OUT_CUTS, seg_width)
    nodes = experts // EXP_GROUP
    replica = lax.axis_index("replica")
    node = lax.axis_index("node")
    local = lax.axis_index("local")
    sharer = lax.rem(local, sharers)
    mine = node * EXP_GROUP + lax.div(local, sharers)

    def at_expert(expert, share):
        return (
            replica,
            lax.div(expert, EXP_GROUP),
            lax.rem(expert, EXP_GROUP) * sharers + share,
        )

    def other_expert(step):
        return lax.rem(mine + step + experts, experts)

    away = [step for step in range(1, experts) if step % EXP_GROUP]
    away.sort(key=lambda step: min(step % EXP_GROUP, -step % EXP_GROUP))
    here = [step for step in range(EXP_GROUP, experts, EXP_GROUP)]

    def other_sharer(step):
        return lax.rem(sharer + step, sharers)

    def weight_copy(kind, chunk, seg):
        offset, width = (out_spans if kind == 2 else row_spans)[chunk]
        held = pl.ds(SEGS * offset + seg * width, width)
        taken = pl.ds(seg * seg_width + offset, width)
        if kind == 2:
            source, target = down_hbm.at[:, taken], down_w.at[:, held]
        else:
            source = (gate_hbm, up_hbm)[kind].at[taken, :]
            target = (gate_w, up_w)[kind].at[held, :]
        return pltpu.make_async_copy(source, target, w_sem.at[kind, chunk, seg])

    for chunk in range(len(row_spans)):
        for kind in range(2):
            for seg in range(SEGS):
                weight_copy(kind, chunk, seg).start()
    for chunk in range(len(out_spans)):
        for seg in range(SEGS):
            weight_copy(2, chunk, seg).start()

    barrier = pltpu.get_barrier_semaphore()
    for step in range(1, experts):
        pl.semaphore_signal(
            barrier, inc=1, device_id=at_expert(other_expert(step), sharer), device_id_type=MESH
        )
    for step in range(1, sharers):
        pl.semaphore_signal(
            barrier, inc=1, device_id=at_expert(mine, other_sharer(step)), device_id_type=MESH
        )
        for ahead in here:
            pl.semaphore_signal(
                barrier,
                inc=1,
                device_id=at_expert(other_expert(ahead), other_sharer(step)),
                device_id_type=MESH,
            )

    shape = (flat, 2 * SEGS * PAD_ROWS)
    lanes = shape[1]
    spread = (iota((row_count, lanes), 0) == iota((row_count, lanes), 1) % PAD_ROWS).astype(F32)
    named = jnp.dot(ids_ref[...].astype(F32), spread, preferred_element_type=F32)
    shares = jnp.dot(
        weight_ref[...], spread, precision=lax.Precision.HIGHEST, preferred_element_type=F32
    )
    expert = (iota(shape, 0) // slots).astype(F32)
    lane_row = iota(shape, 1) % PAD_ROWS
    chosen = jnp.zeros(shape, F32)
    weights = jnp.zeros(shape, F32)
    for route in range(routes):
        same = (named[route:route + 1, :] == expert) & (lane_row < row_count)
        chosen = jnp.where(same, 1.0, chosen)
        weights = jnp.where(same, shares[route:route + 1, :], weights)
    first, second = iota((lanes, lanes), 0), iota((lanes, lanes), 1)
    earlier = (first // PAD_ROWS == second // PAD_ROWS) & (first < second)
    before = jnp.dot(
        chosen.astype(BF16), earlier.astype(F32).astype(BF16), preferred_element_type=F32
    )
    same_seg = (iota(shape, 0) // CAPACITY) % SEGS == iota(shape, 1) // PAD_ROWS
    fills = (before == (iota(shape, 0) % CAPACITY).astype(F32)) & same_seg
    hit = jnp.where(fills, chosen, 0.0)
    mixing[...] = jnp.where(fills, weights, 0.0)
    picked = hit.astype(BF16)[:, :SEGS * PAD_ROWS]

    values = hidden_ref[...].astype(F32)
    scale = lax.rsqrt(jnp.mean(values * values, axis=1, keepdims=True) + 1e-06)
    normed = values * scale * gain_ref[...]
    stacked[...] = jnp.zeros_like(stacked)
    for seg in range(SEGS):
        stacked[pl.ds(seg * PAD_ROWS, row_count), :] = normed[
            :, seg * seg_width:(seg + 1) * seg_width
        ]

    def columns(span):
        return pl.ds(span[0], span[1])

    def row_copy(chunk, source_expert, target_expert, source_share, target_share):
        span = columns(row_spans[chunk])
        return pltpu.make_async_remote_copy(
            src_ref=outbox.at[target_expert, :, span],
            dst_ref=inbox.at[source_share, source_expert, :, span],
            send_sem=row_send.at[chunk, target_share, target_expert],
            recv_sem=row_recv.at[chunk, source_share, source_expert],
            device_id=at_expert(target_expert, target_share),
            device_id_type=MESH,
        )

    def forward_copy(chunk, source_expert, target_share):
        span = columns(row_spans[chunk])
        return pltpu.make_async_remote_copy(
            src_ref=inbox.at[sharer, source_expert, :, span],
            dst_ref=inbox.at[sharer, source_expert, :, span],
            send_sem=fwd_send.at[chunk, target_share, source_expert],
            recv_sem=row_recv.at[chunk, sharer, source_expert],
            device_id=at_expert(mine, target_share),
            device_id_type=MESH,
        )

    def part_copy(chunk, source_share, target_share):
        return pltpu.make_async_remote_copy(
            src_ref=part_out.at[target_share, :, columns(out_spans[chunk])],
            dst_ref=part_in.at[source_share, :, columns(out_spans[chunk])],
            send_sem=part_send.at[chunk, target_share],
            recv_sem=part_recv.at[chunk, source_share],
            device_id=at_expert(mine, target_share),
            device_id_type=MESH,
        )

    def sum_copy(chunk, source_expert, target_expert):
        return pltpu.make_async_remote_copy(
            src_ref=sum_out.at[target_expert, :, columns(out_spans[chunk])],
            dst_ref=sum_in.at[source_expert, :, columns(out_spans[chunk])],
            send_sem=sum_send.at[chunk, target_expert],
            recv_sem=sum_recv.at[chunk, source_expert],
            device_id=at_expert(target_expert, sharer),
            device_id_type=MESH,
        )

    pl.semaphore_wait(barrier, experts - 1 + nodes * (sharers - 1))

    def place(chunk):
        offset, width = row_spans[chunk]
        rows = stacked[:, offset:offset + width].astype(BF16)
        placed = jnp.dot(picked, rows, preferred_element_type=F32).astype(BF16)
        outbox[:, :, offset:offset + width] = placed.reshape(experts, slots, width)
        for step in away:
            row_copy(chunk, mine, other_expert(step), sharer, sharer).start()
        for turn in range(1, sharers):
            row_copy(chunk, mine, mine, sharer, other_sharer(turn)).start()
            for step in here:
                row_copy(chunk, mine, other_expert(step), sharer, other_sharer(turn)).start()
        for step in here:
            row_copy(chunk, mine, other_expert(step), sharer, sharer).start()
        inbox[sharer, mine, :, offset:offset + width] = outbox[mine, :, offset:offset + width]

    to_segments = one_hot_shuffle(experts, True)
    to_experts = one_hot_shuffle(experts, False)

    def arrive(chunk, source, share):
        row_copy(chunk, source, source, share, share).wait_recv()

    def gather_rows(chunk):
        for step in away:
            source = other_expert(-step)
            arrive(chunk, source, sharer)
            for turn in range(1, sharers):
                forward_copy(chunk, source, other_sharer(turn)).start()
        for step in here:
            arrive(chunk, other_expert(-step), sharer)

    def expand(chunk):
        offset, width = row_spans[chunk]
        for turn in range(1, sharers):
            for source in range(experts):
                arrive(chunk, source, other_sharer(turn))
        for share in range(sharers):
            ordered = jnp.dot(
                to_segments,
                inbox[share, :, :, offset:offset + width].reshape(flat, width),
                preferred_element_type=F32,
            ).astype(BF16)
            for seg in range(SEGS):
                at = SEGS * offset + seg * width
                rows_in[share * block:(share + 1) * block, at:at + width] = (
                    ordered[seg * block:(seg + 1) * block]
                )
        held = slice(SEGS * offset, SEGS * (offset + width))
        for kind, matrix, total in ((0, gate_w, gate_acc), (1, up_w, up_acc)):
            for seg in range(SEGS):
                weight_copy(kind, chunk, seg).wait()
            product = jnp.dot(rows_in[:, held], matrix[held], preferred_element_type=F32)
            if chunk == 0:
                total[...] = product
            else:
                total[...] += product

    for chunk in range(len(row_spans)):
        place(chunk)
    for chunk in range(len(row_spans)):
        gather_rows(chunk)
        if chunk >= 1:
            expand(chunk - 1)
    expand(len(row_spans) - 1)

    gate = gate_acc[...]
    active = (gate / (1.0 + jnp.exp(-gate)) * up_acc[...]).astype(BF16)

    mix = jnp.transpose(mixing[...])[:SEGS * PAD_ROWS]
    mix_high = mix.astype(BF16)
    rest = mix - mix_high.astype(F32)
    mix_mid = rest.astype(BF16)
    mix_low = (rest - mix_mid.astype(F32)).astype(BF16)
    mix_parts = jnp.concatenate([mix_high, mix_mid, mix_low], axis=0)

    def contract(chunk):
        offset, width = out_spans[chunk]
        for seg in range(SEGS):
            weight_copy(2, chunk, seg).wait()
        product = jnp.dot(
            active,
            down_w[:, SEGS * offset:SEGS * (offset + width)],
            preferred_element_type=F32,
        ).astype(BF16)
        for share in range(sharers):
            for seg in range(SEGS):
                part_out[share, seg * block:(seg + 1) * block, offset:offset + width] = product[
                    share * block:(share + 1) * block, seg * width:(seg + 1) * width
                ]
        for step in range(1, sharers):
            if chunk >= IN_FLIGHT:
                part_copy(chunk - IN_FLIGHT, sharer, other_sharer(step)).wait_send()
            part_copy(chunk, sharer, other_sharer(step)).start()

    def add_parts(chunk):
        offset, width = out_spans[chunk]
        total = part_out[sharer, :, offset:offset + width].astype(F32)
        for step in range(1, sharers):
            source = other_sharer(step)
            part_copy(chunk, source, source).wait_recv()
            total = total + part_in[source, :, offset:offset + width].astype(F32)
        ordered = jnp.dot(to_experts, total.astype(BF16), preferred_element_type=F32).astype(BF16)
        sum_out[:, :, offset:offset + width] = ordered.reshape(experts, slots, width)
        for step in away + here:
            sum_copy(chunk, mine, other_expert(step)).start()
        sum_in[mine, :, offset:offset + width] = sum_out[mine, :, offset:offset + width]

    def mix_rows(chunk):
        offset, width = out_spans[chunk]
        for step in away + here:
            source = other_expert(-step)
            sum_copy(chunk, source, source).wait_recv()
        arrived = sum_in[:, :, offset:offset + width].reshape(flat, width)
        terms = jnp.dot(mix_parts, arrived, preferred_element_type=F32)
        size = SEGS * PAD_ROWS
        mixed = terms[:size] + terms[size:2 * size] + terms[2 * size:]
        for seg in range(SEGS):
            at = seg * seg_width + offset
            out_ref[:, at:at + width] = mixed[
                seg * PAD_ROWS:seg * PAD_ROWS + row_count
            ].astype(BF16)

    count = len(out_spans)
    for turn in range(count + MIX_LAG):
        if turn < count:
            contract(turn)
        if 0 <= turn - ADD_LAG < count:
            add_parts(turn - ADD_LAG)
        if 0 <= turn - MIX_LAG < count:
            mix_rows(turn - MIX_LAG)

    for chunk in range(len(row_spans)):
        for step in away + here:
            row_copy(chunk, mine, other_expert(step), sharer, sharer).wait_send()
        for turn in range(1, sharers):
            share = other_sharer(turn)
            for step in [0] + here:
                row_copy(chunk, mine, other_expert(step), sharer, share).wait_send()
            for step in away:
                forward_copy(chunk, other_expert(-step), share).wait_send()
    for chunk in range(count):
        for step in away + here:
            sum_copy(chunk, mine, other_expert(step)).wait_send()
        if chunk >= count - IN_FLIGHT:
            for step in range(1, sharers):
                part_copy(chunk, sharer, other_sharer(step)).wait_send()


def shards(hidden, norm_gain, expert_ids, gate_weight, gate_proj, up_proj, down_proj):
    experts = EXP_GROUP * lax.axis_size("node")
    sharers = lax.axis_size("local") // EXP_GROUP
    row_count, model_width = hidden.shape
    routes = expert_ids.shape[1]
    units = gate_proj.shape[1]
    seg_width = model_width // SEGS
    row_chunks, out_chunks = len(ROW_CUTS), len(OUT_CUTS)
    slots = SEGS * CAPACITY
    flat = experts * slots
    block = experts * CAPACITY
    vmem = pl.BlockSpec(memory_space=pltpu.VMEM)
    anywhere = pl.BlockSpec(memory_space=pl.ANY)
    dma = pltpu.SemaphoreType.DMA
    return pl.pallas_call(
        functools.partial(kernel, (experts, sharers, row_count, routes)),
        out_shape=jax.ShapeDtypeStruct((row_count, model_width), BF16),
        in_specs=[vmem] * 4 + [anywhere] * 3,
        out_specs=vmem,
        scratch_shapes=[
            pltpu.VMEM((model_width, units), BF16),
            pltpu.VMEM((model_width, units), BF16),
            pltpu.VMEM((units, model_width), BF16),
            pltpu.VMEM((SEGS * PAD_ROWS, seg_width), F32),
            pltpu.VMEM((flat, 2 * SEGS * PAD_ROWS), F32),
            pltpu.VMEM((experts, slots, seg_width), BF16),
            pltpu.VMEM((sharers, experts, slots, seg_width), BF16),
            pltpu.VMEM((sharers * block, model_width), BF16),
            pltpu.VMEM((sharers * block, units), F32),
            pltpu.VMEM((sharers * block, units), F32),
            pltpu.VMEM((sharers, SEGS * block, seg_width), BF16),
            pltpu.VMEM((sharers, SEGS * block, seg_width), BF16),
            pltpu.VMEM((experts, slots, seg_width), BF16),
            pltpu.VMEM((experts, slots, seg_width), BF16),
            dma((3, max(row_chunks, out_chunks), SEGS)),
            dma((row_chunks, sharers, experts)),
            dma((row_chunks, sharers, experts)),
            dma((row_chunks, sharers, experts)),
            dma((out_chunks, sharers)),
            dma((out_chunks, sharers)),
            dma((out_chunks, experts)),
            dma((out_chunks, experts)),
        ],
        compiler_params=pltpu.CompilerParams(
            collective_id=0, has_side_effects=True, vmem_limit_bytes=58 * 1024 * 1024
        ),
        name="expert_layer",
    )(hidden, norm_gain.reshape(1, model_width), expert_ids.T, gate_weight.T, gate_proj, up_proj, down_proj)


def solution(mesh):
    return jax.shard_map(
        shards,
        mesh=mesh,
        in_specs=(
            P(("replica", "node", "local"), None),
            P(),
            P(("replica", "node", "local"), None),
            P(("replica", "node", "local"), None),
            P(None, ("node", "local")),
            P(None, ("node", "local")),
            P(("node", "local"), None),
        ),
        out_specs=P(("replica", "node", "local"), None),
        check_vma=False,
    )
```

```python
import functools

import jax
import jax.numpy as jnp
from jax import lax
from jax.experimental import pallas as pl
from jax.experimental.pallas import tpu as pltpu
from jax.sharding import PartitionSpec as P

EXP_GROUP = 4
CAPACITY = 4
SEGS = 4
PAD_ROWS = 16
IN_FLIGHT = 2
ADD_LAG = 2
MIX_LAG = 4
ROW_CUTS = (9, 5)
OUT_CUTS = (4, 4, 4, 2)
MESH = pl.DeviceIdType.MESH
F32 = jnp.float32
BF16 = jnp.bfloat16


def iota(shape, dim):
    return lax.broadcasted_iota(jnp.int32, shape, dim)


def spans(cuts, whole):
    unit, at, out = whole // sum(cuts), 0, []
    for cut in cuts:
        out.append((at, cut * unit))
        at += cut * unit
    return out


def one_hot_shuffle(experts, to_segments):
    rows = experts * SEGS * CAPACITY
    first, second = iota((rows, rows), 0), iota((rows, rows), 1)
    by_segment, by_expert = (first, second) if to_segments else (second, first)
    expert = by_expert // (SEGS * CAPACITY)
    segment = (by_expert // CAPACITY) % SEGS
    slot = by_expert % CAPACITY
    wanted = segment * (experts * CAPACITY) + expert * CAPACITY + slot
    return (by_segment == wanted).astype(F32).astype(BF16)


def kernel(
    dims,
    hidden_ref, gain_ref, ids_ref, weight_ref, gate_hbm, up_hbm, down_hbm,
    out_ref,
    gate_w, up_w, down_w, stacked, mixing, outbox, inbox, rows_in, gate_acc, up_acc,
    part_out, part_in, sum_out, sum_in,
    w_sem, row_send, row_recv, fwd_send, part_send, part_recv, sum_send, sum_recv,
):
    experts, sharers, row_count, routes = dims
    slots = SEGS * CAPACITY
    flat = experts * slots
    block = experts * CAPACITY
    model_width = hidden_ref.shape[1]
    seg_width = model_width // SEGS
    row_spans, out_spans = spans(ROW_CUTS, seg_width), spans(OUT_CUTS, seg_width)
    nodes = experts // EXP_GROUP
    replica = lax.axis_index("replica")
    node = lax.axis_index("node")
    local = lax.axis_index("local")
    sharer = lax.rem(local, sharers)
    mine = node * EXP_GROUP + lax.div(local, sharers)

    def at_expert(expert, share):
        return (
            replica,
            lax.div(expert, EXP_GROUP),
            lax.rem(expert, EXP_GROUP) * sharers + share,
        )

    def other_expert(step):
        return lax.rem(mine + step + experts, experts)

    away = [step for step in range(1, experts) if step % EXP_GROUP]
    away.sort(key=lambda step: min(step % EXP_GROUP, -step % EXP_GROUP))
    here = [step for step in range(EXP_GROUP, experts, EXP_GROUP)]

    def other_sharer(step):
        return lax.rem(sharer + step, sharers)

    def weight_copy(kind, chunk, seg):
        offset, width = (out_spans if kind == 2 else row_spans)[chunk]
        held = pl.ds(SEGS * offset + seg * width, width)
        taken = pl.ds(seg * seg_width + offset, width)
        if kind == 2:
            source, target = down_hbm.at[:, taken], down_w.at[:, held]
        else:
            source = (gate_hbm, up_hbm)[kind].at[taken, :]
            target = (gate_w, up_w)[kind].at[held, :]
        return pltpu.make_async_copy(source, target, w_sem.at[kind, chunk, seg])

    for chunk in range(len(row_spans)):
        for kind in range(2):
            for seg in range(SEGS):
                weight_copy(kind, chunk, seg).start()
    for chunk in range(len(out_spans)):
        for seg in range(SEGS):
            weight_copy(2, chunk, seg).start()

    barrier = pltpu.get_barrier_semaphore()
    for step in range(1, experts):
        pl.semaphore_signal(
            barrier, inc=1, device_id=at_expert(other_expert(step), sharer), device_id_type=MESH
        )
    for step in range(1, sharers):
        pl.semaphore_signal(
            barrier, inc=1, device_id=at_expert(mine, other_sharer(step)), device_id_type=MESH
        )
        for ahead in here:
            pl.semaphore_signal(
                barrier,
                inc=1,
                device_id=at_expert(other_expert(ahead), other_sharer(step)),
                device_id_type=MESH,
            )

    shape = (flat, 2 * SEGS * PAD_ROWS)
    lanes = shape[1]
    spread = (iota((row_count, lanes), 0) == iota((row_count, lanes), 1) % PAD_ROWS).astype(F32)
    named = jnp.dot(ids_ref[...].astype(F32), spread, preferred_element_type=F32)
    shares = jnp.dot(
        weight_ref[...], spread, precision=lax.Precision.HIGHEST, preferred_element_type=F32
    )
    expert = (iota(shape, 0) // slots).astype(F32)
    lane_row = iota(shape, 1) % PAD_ROWS
    chosen = jnp.zeros(shape, F32)
    weights = jnp.zeros(shape, F32)
    for route in range(routes):
        same = (named[route:route + 1, :] == expert) & (lane_row < row_count)
        chosen = jnp.where(same, 1.0, chosen)
        weights = jnp.where(same, shares[route:route + 1, :], weights)
    first, second = iota((lanes, lanes), 0), iota((lanes, lanes), 1)
    earlier = (first // PAD_ROWS == second // PAD_ROWS) & (first < second)
    before = jnp.dot(
        chosen.astype(BF16), earlier.astype(F32).astype(BF16), preferred_element_type=F32
    )
    same_seg = (iota(shape, 0) // CAPACITY) % SEGS == iota(shape, 1) // PAD_ROWS
    fills = (before == (iota(shape, 0) % CAPACITY).astype(F32)) & same_seg
    hit = jnp.where(fills, chosen, 0.0)
    mixing[...] = jnp.where(fills, weights, 0.0)
    picked = hit.astype(BF16)[:, :SEGS * PAD_ROWS]

    values = hidden_ref[...].astype(F32)
    scale = lax.rsqrt(jnp.mean(values * values, axis=1, keepdims=True) + 1e-06)
    normed = values * scale * gain_ref[...]
    stacked[...] = jnp.zeros_like(stacked)
    for seg in range(SEGS):
        stacked[pl.ds(seg * PAD_ROWS, row_count), :] = normed[
            :, seg * seg_width:(seg + 1) * seg_width
        ]

    def columns(span):
        return pl.ds(span[0], span[1])

    def row_copy(chunk, source_expert, target_expert, source_share, target_share):
        span = columns(row_spans[chunk])
        return pltpu.make_async_remote_copy(
            src_ref=outbox.at[target_expert, :, span],
            dst_ref=inbox.at[source_share, source_expert, :, span],
            send_sem=row_send.at[chunk, target_share, target_expert],
            recv_sem=row_recv.at[chunk, source_share, source_expert],
            device_id=at_expert(target_expert, target_share),
            device_id_type=MESH,
        )

    def forward_copy(chunk, source_expert, target_share):
        span = columns(row_spans[chunk])
        return pltpu.make_async_remote_copy(
            src_ref=inbox.at[sharer, source_expert, :, span],
            dst_ref=inbox.at[sharer, source_expert, :, span],
            send_sem=fwd_send.at[chunk, target_share, source_expert],
            recv_sem=row_recv.at[chunk, sharer, source_expert],
            device_id=at_expert(mine, target_share),
            device_id_type=MESH,
        )

    def part_copy(chunk, source_share, target_share):
        return pltpu.make_async_remote_copy(
            src_ref=part_out.at[target_share, :, columns(out_spans[chunk])],
            dst_ref=part_in.at[source_share, :, columns(out_spans[chunk])],
            send_sem=part_send.at[chunk, target_share],
            recv_sem=part_recv.at[chunk, source_share],
            device_id=at_expert(mine, target_share),
            device_id_type=MESH,
        )

    def sum_copy(chunk, source_expert, target_expert):
        return pltpu.make_async_remote_copy(
            src_ref=sum_out.at[target_expert, :, columns(out_spans[chunk])],
            dst_ref=sum_in.at[source_expert, :, columns(out_spans[chunk])],
            send_sem=sum_send.at[chunk, target_expert],
            recv_sem=sum_recv.at[chunk, source_expert],
            device_id=at_expert(target_expert, sharer),
            device_id_type=MESH,
        )

    pl.semaphore_wait(barrier, experts - 1 + nodes * (sharers - 1))

    def place(chunk):
        offset, width = row_spans[chunk]
        rows = stacked[:, offset:offset + width].astype(BF16)
        placed = jnp.dot(picked, rows, preferred_element_type=F32).astype(BF16)
        outbox[:, :, offset:offset + width] = placed.reshape(experts, slots, width)
        for step in away:
            row_copy(chunk, mine, other_expert(step), sharer, sharer).start()
        for turn in range(1, sharers):
            row_copy(chunk, mine, mine, sharer, other_sharer(turn)).start()
            for step in here:
                row_copy(chunk, mine, other_expert(step), sharer, other_sharer(turn)).start()
        for step in here:
            row_copy(chunk, mine, other_expert(step), sharer, sharer).start()
        inbox[sharer, mine, :, offset:offset + width] = outbox[mine, :, offset:offset + width]

    to_segments = one_hot_shuffle(experts, True)
    to_experts = one_hot_shuffle(experts, False)

    def arrive(chunk, source, share):
        row_copy(chunk, source, source, share, share).wait_recv()

    def gather_rows(chunk):
        for step in away:
            source = other_expert(-step)
            arrive(chunk, source, sharer)
            for turn in range(1, sharers):
                forward_copy(chunk, source, other_sharer(turn)).start()
        for step in here:
            arrive(chunk, other_expert(-step), sharer)

    def expand(chunk):
        offset, width = row_spans[chunk]
        for turn in range(1, sharers):
            for source in range(experts):
                arrive(chunk, source, other_sharer(turn))
        for share in range(sharers):
            ordered = jnp.dot(
                to_segments,
                inbox[share, :, :, offset:offset + width].reshape(flat, width),
                preferred_element_type=F32,
            ).astype(BF16)
            for seg in range(SEGS):
                at = SEGS * offset + seg * width
                rows_in[share * block:(share + 1) * block, at:at + width] = (
                    ordered[seg * block:(seg + 1) * block]
                )
        held = slice(SEGS * offset, SEGS * (offset + width))
        for kind, matrix, total in ((0, gate_w, gate_acc), (1, up_w, up_acc)):
            for seg in range(SEGS):
                weight_copy(kind, chunk, seg).wait()
            product = jnp.dot(rows_in[:, held], matrix[held], preferred_element_type=F32)
            if chunk == 0:
                total[...] = product
            else:
                total[...] += product

    for chunk in range(len(row_spans)):
        place(chunk)
    for chunk in range(len(row_spans)):
        gather_rows(chunk)
        if chunk >= 1:
            expand(chunk - 1)
    expand(len(row_spans) - 1)

    gate = gate_acc[...]
    active = (gate / (1.0 + jnp.exp(-gate)) * up_acc[...]).astype(BF16)

    mix = jnp.transpose(mixing[...])[:SEGS * PAD_ROWS]
    mix_high = mix.astype(BF16)
    rest = mix - mix_high.astype(F32)
    mix_mid = rest.astype(BF16)
    mix_low = (rest - mix_mid.astype(F32)).astype(BF16)
    mix_parts = jnp.concatenate([mix_high, mix_mid, mix_low], axis=0)

    def contract(chunk):
        offset, width = out_spans[chunk]
        for seg in range(SEGS):
            weight_copy(2, chunk, seg).wait()
        product = jnp.dot(
            active,
            down_w[:, SEGS * offset:SEGS * (offset + width)],
            preferred_element_type=F32,
        ).astype(BF16)
        for share in range(sharers):
            for seg in range(SEGS):
                part_out[share, seg * block:(seg + 1) * block, offset:offset + width] = product[
                    share * block:(share + 1) * block, seg * width:(seg + 1) * width
                ]
        for step in range(1, sharers):
            if chunk >= IN_FLIGHT:
                part_copy(chunk - IN_FLIGHT, sharer, other_sharer(step)).wait_send()
            part_copy(chunk, sharer, other_sharer(step)).start()

    def add_parts(chunk):
        offset, width = out_spans[chunk]
        total = part_out[sharer, :, offset:offset + width].astype(F32)
        for step in range(1, sharers):
            source = other_sharer(step)
            part_copy(chunk, source, source).wait_recv()
            total = total + part_in[source, :, offset:offset + width].astype(F32)
        ordered = jnp.dot(to_experts, total.astype(BF16), preferred_element_type=F32).astype(BF16)
        sum_out[:, :, offset:offset + width] = ordered.reshape(experts, slots, width)
        for step in away + here:
            sum_copy(chunk, mine, other_expert(step)).start()
        sum_in[mine, :, offset:offset + width] = sum_out[mine, :, offset:offset + width]

    def mix_rows(chunk):
        offset, width = out_spans[chunk]
        for step in away + here:
            source = other_expert(-step)
            sum_copy(chunk, source, source).wait_recv()
        arrived = sum_in[:, :, offset:offset + width].reshape(flat, width)
        terms = jnp.dot(mix_parts, arrived, preferred_element_type=F32)
        size = SEGS * PAD_ROWS
        mixed = terms[:size] + terms[size:2 * size] + terms[2 * size:]
        for seg in range(SEGS):
            at = seg * seg_width + offset
            out_ref[:, at:at + width] = mixed[
                seg * PAD_ROWS:seg * PAD_ROWS + row_count
            ].astype(BF16)

    count = len(out_spans)
    for turn in range(count + MIX_LAG):
        if turn < count:
            contract(turn)
        if 0 <= turn - ADD_LAG < count:
            add_parts(turn - ADD_LAG)
        if 0 <= turn - MIX_LAG < count:
            mix_rows(turn - MIX_LAG)

    for chunk in range(len(row_spans)):
        for step in away + here:
            row_copy(chunk, mine, other_expert(step), sharer, sharer).wait_send()
        for turn in range(1, sharers):
            share = other_sharer(turn)
            for step in [0] + here:
                row_copy(chunk, mine, other_expert(step), sharer, share).wait_send()
            for step in away:
                forward_copy(chunk, other_expert(-step), share).wait_send()
    for chunk in range(count):
        for step in away + here:
            sum_copy(chunk, mine, other_expert(step)).wait_send()
        if chunk >= count - IN_FLIGHT:
            for step in range(1, sharers):
                part_copy(chunk, sharer, other_sharer(step)).wait_send()


def shards(hidden, norm_gain, expert_ids, gate_weight, gate_proj, up_proj, down_proj):
    experts = EXP_GROUP * lax.axis_size("node")
    sharers = lax.axis_size("local") // EXP_GROUP
    row_count, model_width = hidden.shape
    routes = expert_ids.shape[1]
    units = gate_proj.shape[1]
    seg_width = model_width // SEGS
    row_chunks, out_chunks = len(ROW_CUTS), len(OUT_CUTS)
    slots = SEGS * CAPACITY
    flat = experts * slots
    block = experts * CAPACITY
    vmem = pl.BlockSpec(memory_space=pltpu.VMEM)
    anywhere = pl.BlockSpec(memory_space=pl.ANY)
    dma = pltpu.SemaphoreType.DMA
    return pl.pallas_call(
        functools.partial(kernel, (experts, sharers, row_count, routes)),
        out_shape=jax.ShapeDtypeStruct((row_count, model_width), BF16),
        in_specs=[vmem] * 4 + [anywhere] * 3,
        out_specs=vmem,
        scratch_shapes=[
            pltpu.VMEM((model_width, units), BF16),
            pltpu.VMEM((model_width, units), BF16),
            pltpu.VMEM((units, model_width), BF16),
            pltpu.VMEM((SEGS * PAD_ROWS, seg_width), F32),
            pltpu.VMEM((flat, 2 * SEGS * PAD_ROWS), F32),
            pltpu.VMEM((experts, slots, seg_width), BF16),
            pltpu.VMEM((sharers, experts, slots, seg_width), BF16),
            pltpu.VMEM((sharers * block, model_width), BF16),
            pltpu.VMEM((sharers * block, units), F32),
            pltpu.VMEM((sharers * block, units), F32),
            pltpu.VMEM((sharers, SEGS * block, seg_width), BF16),
            pltpu.VMEM((sharers, SEGS * block, seg_width), BF16),
            pltpu.VMEM((experts, slots, seg_width), BF16),
            pltpu.VMEM((experts, slots, seg_width), BF16),
            dma((3, max(row_chunks, out_chunks), SEGS)),
            dma((row_chunks, sharers, experts)),
            dma((row_chunks, sharers, experts)),
            dma((row_chunks, sharers, experts)),
            dma((out_chunks, sharers)),
            dma((out_chunks, sharers)),
            dma((out_chunks, experts)),
            dma((out_chunks, experts)),
        ],
        compiler_params=pltpu.CompilerParams(
            collective_id=0, has_side_effects=True, vmem_limit_bytes=58 * 1024 * 1024
        ),
        name="expert_layer",
    )(hidden, norm_gain.reshape(1, model_width), expert_ids.T, gate_weight.T, gate_proj, up_proj, down_proj)


def solution(mesh):
    return jax.shard_map(
        shards,
        mesh=mesh,
        in_specs=(
            P(("replica", "node", "local"), None),
            P(),
            P(("replica", "node", "local"), None),
            P(("replica", "node", "local"), None),
            P(None, ("node", "local")),
            P(None, ("node", "local")),
            P(("node", "local"), None),
        ),
        out_specs=P(("replica", "node", "local"), None),
        check_vma=False,
    )
```
